32 devices in a mesh: groups: 2 (over x), tile: 4 (over y, core), led: 4 (over z).
Axes of the slice: x: 2, y: 2, z: 4, core: 2. Of those that a mesh axis runs over, the one named last changes fastest.
Arguments:
- spectra: bfloat16 [16, 2, 384, 384], P(('groups', 'tile')), parts along dimension 0, may hold values from -6 to 6
- pupils: float32 [16, 2, 256, 256], P(('groups', 'tile')), parts along dimension 0, may hold values from -3 to 3
- amplitudes: bfloat16 [16, 8, 256, 256], P(('groups', 'tile'), 'led'), parts along dimension 0, may hold values from 0.19921875 to 2
- offsets: int32 [16, 8, 2], P(('groups', 'tile'), 'led'), parts along dimension 0, may hold values from 0 to 128
- positions: int32 [16, 2], P(('groups', 'tile')), parts along dimension 0, may hold values from 0 to 2047
Outputs:
- refitted: float32 [16, 2, 256, 256], P(('groups', 'tile'), None, 'led'), parts along dimension 0
The draws below stay inside these ranges and needn't reach their ends.
There are 2 independent parts, one for each index of `groups`. The reference program is written for one: setup_inputs(seed, part) draws one part's arguments, and reference() takes and returns one part's arrays. A program takes and returns all parts, laid end to end along the dimension named above; each array names one. Nothing has to cross between parts.
Inputs may be any that keep to these rules, and one draw needn't show every extreme that they name: `offsets`: every sub-spectrum lies inside its tile's spectrum.
All inputs are finite; a program needn't handle non-finite values.
Results may differ from the reference program's by a relative error of at most 0.0022.
Values sent between devices are 32-bit elements; how exact they have to be, the bound alone decides.
A program may use at most 64 MiB of HBM per device.

```python
import math
import jax
import jax.numpy as jnp
from jax import lax

PS = 256
SHIFT = 128
OS = 384
DEG = 5
FIELD = 2048
TILES = 8
LEDS = 8


def with_ends(values, stream_key, low, top_value):
    longest = values.shape.index(max(values.shape))
    spots = []
    for shift in (0, 1):
        where = [jax.random.randint(jax.random.fold_in(stream_key, axis), (), 0, length) for axis, length in enumerate(values.shape)]
        where[longest] = (where[longest] + shift) % values.shape[longest]
        spots.append(tuple(where))
    return values.at[spots[0]].set(low).at[spots[1]].set(top_value)


def shard_levels(stream_key, dims, shards, low, high):
    loudness = 1.0
    for axis_at, parts in shards:
        steps = jax.random.uniform(jax.random.fold_in(jax.random.fold_in(stream_key, 6), axis_at), (parts,), jnp.float32, low / len(shards), high / len(shards))
        loudness = loudness * jnp.repeat(jnp.exp(steps), dims[axis_at] // parts).reshape((-1,) + (1,) * (len(dims) - 1 - axis_at))
    return loudness


def bell_draw(own_key, shape, deviation, limit, cuts=(), kind=jnp.bfloat16):
    array = deviation * jax.random.normal(own_key, shape, jnp.float32)
    if cuts:
        array = array * shard_levels(own_key, shape, cuts, -0.22, 0.18)
    return jnp.clip(array, -limit, limit).astype(kind)


def setup_inputs(seed: int = 0, part: int = 0) -> dict:
    seeds = jax.random.split(jax.random.key(seed), 6)
    part_keys = jax.random.split(jax.random.fold_in(seeds[5], part), 6)
    return {
        "spectra": bell_draw(part_keys[0], (TILES, 2, OS, OS), 1.0, 6.0, ((0, 4),)),
        "pupils": bell_draw(part_keys[1], (TILES, 2, PS, PS), 0.5, 3.0, ((0, 4),), jnp.float32),
        "amplitudes": jnp.clip(jnp.exp(math.log(2.0) - 2.306499 * jax.random.uniform(part_keys[2], (TILES, LEDS, PS, PS), jnp.float32) ** shard_levels(part_keys[2], (TILES, LEDS, PS, PS), ((0, 4), (1, 4)), -0.2, 0.2)), 0.19921875, 2.0).astype(jnp.bfloat16),
        "offsets": with_ends(jax.random.randint(part_keys[3], (TILES, LEDS, 2), 0, SHIFT + 1), jax.random.fold_in(part_keys[3], 1), 0, SHIFT).astype(jnp.int32),
        "positions": with_ends(jax.random.randint(part_keys[4], (TILES, 2), 0, FIELD), jax.random.fold_in(part_keys[4], 1), 0, FIELD - 1).astype(jnp.int32),
    }


RIDGE = 0.05
FLOOR = 0.25

def fourier_tables(length, sign):
    index = jnp.arange(length, dtype=jnp.int32)
    product = index[:, None] * index[None, :] % length
    angle = product.astype(jnp.float32) * (2.0 * math.pi / length)
    factor = 1.0 / math.sqrt(length)
    return ((jnp.cos(angle) * factor).astype(jnp.bfloat16), (sign * jnp.sin(angle) * factor).astype(jnp.bfloat16))

def fourier_square(real_part, imag_part, table_re, table_im):
    length = real_part.shape[0]
    left_side = jnp.concatenate([table_re, table_im], 0)
    right_side = jnp.concatenate([real_part, imag_part], 1)
    first_prod = jnp.dot(left_side.astype(jnp.float32), right_side.astype(jnp.float32), preferred_element_type=jnp.float32)
    middle_re = (first_prod[:length, :length] - first_prod[length:, length:]).astype(jnp.bfloat16)
    middle_im = (first_prod[:length, length:] + first_prod[length:, :length]).astype(jnp.bfloat16)
    left_side = jnp.concatenate([middle_re, middle_im], 0)
    right_side = jnp.concatenate([table_re, table_im], 1)
    second_prod = jnp.dot(left_side.astype(jnp.float32), right_side.astype(jnp.float32), preferred_element_type=jnp.float32)
    result_re = second_prod[:length, :length] - second_prod[length:, length:]
    result_im = second_prod[:length, length:] + second_prod[length:, :length]
    return (result_re, result_im)

def led_update(spectrum, pupil_tile, amplitude, offset, tables):
    length = pupil_tile.shape[1]
    zero_index = jnp.zeros((), jnp.int32)
    window = lax.dynamic_slice(spectrum, (zero_index, offset[0].astype(jnp.int32), offset[1].astype(jnp.int32)), (2, length, length)).astype(jnp.float32)
    window_re, window_im = (window[0], window[1])
    field_re = (pupil_tile[0] * window_re - pupil_tile[1] * window_im).astype(jnp.bfloat16)
    field_im = (pupil_tile[0] * window_im + pupil_tile[1] * window_re).astype(jnp.bfloat16)
    wave_re, wave_im = fourier_square(field_re, field_im, tables[2], tables[3])
    magnitude = jnp.sqrt(wave_re * wave_re + wave_im * wave_im)
    amp_ratio = amplitude.astype(jnp.float32) / jnp.maximum(magnitude, FLOOR) - 1.0
    diff_re = (wave_re * amp_ratio).astype(jnp.bfloat16)
    diff_im = (wave_im * amp_ratio).astype(jnp.bfloat16)
    delta_re, delta_im = fourier_square(diff_re, diff_im, tables[0], tables[1])
    grad_re = window_re * delta_re + window_im * delta_im
    grad_im = window_re * delta_im - window_im * delta_re
    peak_value = jnp.max(window_re * window_re + window_im * window_im)
    return (jnp.stack([grad_re, grad_im]), peak_value)

def tile_pass(spectrum, pupil_tile, amplitude_set, offset_set, tables):

    def advance(carry, items):
        term, peak_value = led_update(spectrum, pupil_tile, items[0], items[1], tables)
        return ((carry[0] + term, carry[1] + peak_value), None)
    start_state = (jnp.zeros(pupil_tile.shape, jnp.float32), jnp.zeros((), jnp.float32))
    final_state, unused = lax.scan(advance, start_state, (amplitude_set, offset_set))
    return final_state

def legendre_basis(positions):
    coords = positions.astype(jnp.float32) * (2.0 / (FIELD - 1)) - 1.0

    def series(values):
        polys = [jnp.ones_like(values), values]
        for degree in range(2, DEG + 1):
            polys.append(((2 * degree - 1) * values * polys[-1] - (degree - 1) * polys[-2]) / degree)
        return polys
    along_x = series(coords[:, 0])
    along_y = series(coords[:, 1])
    columns = [along_x[first] * along_y[order_sum - first] for order_sum in range(DEG + 1) for first in range(order_sum + 1)]
    return jnp.stack(columns, 1)

def reference(spectra, pupils, amplitudes, offsets, positions):
    forward_re, forward_im = fourier_tables(PS, -1.0)
    inverse_re, inverse_im = fourier_tables(PS, 1.0)
    tables = (forward_re, forward_im, inverse_re, inverse_im)
    gradient, peak_sums = lax.map(lambda items: tile_pass(items[0], items[1], items[2], items[3], tables), (spectra, pupils, amplitudes, offsets))
    updated = pupils + gradient / (peak_sums / LEDS)[:, None, None, None]
    basis_rows = legendre_basis(positions)
    term_count = basis_rows.shape[1]
    gram_matrix = jnp.dot(basis_rows.T.astype(jnp.float32), basis_rows.astype(jnp.float32), precision=lax.Precision.HIGHEST, preferred_element_type=jnp.float32)
    gram_matrix = gram_matrix + RIDGE * TILES * jnp.eye(term_count, dtype=jnp.float32)
    projection = jnp.einsum('tk,tcuv->kcuv', basis_rows, updated, precision=lax.Precision.HIGHEST)
    factor = jnp.linalg.cholesky(gram_matrix)
    pupil_maps = jax.scipy.linalg.cho_solve((factor, True), projection.reshape(term_count, -1)).reshape(projection.shape)
    return jnp.einsum('tk,kcuv->tcuv', basis_rows, pupil_maps, precision=lax.Precision.HIGHEST)
```

```python
import functools
import math

import jax
import jax.numpy as jnp
import numpy as np
from jax import lax
from jax.experimental import pallas as pl
from jax.experimental.pallas import tpu as pltpu
from jax.sharding import PartitionSpec as P

DEG = 5
FIELD = 2048
RIDGE = 0.05
FLOOR = 0.25
MESH = pl.DeviceIdType.MESH


def inverse_tables(length):
    index = np.arange(length, dtype=np.int64)
    angle = (index[:, None] * index[None, :] % length) * (2.0 * math.pi / length)
    factor = 1.0 / math.sqrt(length)
    real_part = (np.cos(angle) * factor).astype(np.float32)
    imag_part = (np.sin(angle) * factor).astype(np.float32)
    first = np.block([[real_part, -imag_part], [imag_part, real_part]])
    second = np.block([[real_part, imag_part], [-imag_part, real_part]])
    return first.astype(jnp.bfloat16), second.astype(jnp.bfloat16)


def legendre(values):
    polys = [jnp.ones_like(values), values]
    for degree in range(2, DEG + 1):
        polys.append(((2 * degree - 1) * values * polys[-1] - (degree - 1) * polys[-2]) / degree)
    return polys


def mixing_matrix(place_rows, tiles):
    lanes = lax.broadcasted_iota(jnp.int32, (tiles, 128), 1)
    subs = lax.broadcasted_iota(jnp.int32, (tiles, 128), 0)
    ridge = RIDGE * tiles
    products = []
    for axis in range(2):
        down = jnp.zeros((tiles, 128), jnp.float32)
        along = jnp.zeros((tiles, 128), jnp.float32)
        for tile in range(tiles):
            row = jnp.broadcast_to(place_rows[tile][axis], (tiles, 128))
            down = jnp.where(subs == tile, row, down)
            along = jnp.where(lanes == tile, row, along)
        scale = 2.0 / (FIELD - 1)
        down, along = (down * scale - 1.0, along * scale - 1.0)
        products.append([a * b for a, b in zip(legendre(down), legendre(along))])
    kernel = jnp.zeros((tiles, 128), jnp.float32)
    partial = jnp.zeros((tiles, 128), jnp.float32)
    for degree in range(DEG + 1):
        partial = partial + products[1][degree]
        kernel = kernel + products[0][DEG - degree] * partial
    eye = jnp.where(subs == lanes, 1.0, 0.0)
    left = kernel + ridge * eye
    right = eye
    for step in range(tiles):
        pivot_row = left[step : step + 1, :]
        pivot = jnp.sum(jnp.where(lanes[:1] == step, pivot_row, 0.0), axis=1, keepdims=True)
        column = jnp.sum(jnp.where(lanes == step, left, 0.0), axis=1, keepdims=True)
        factor = jnp.where(subs[:, :1] == step, 1.0 - 1.0 / pivot, column / pivot)
        left = left - factor * pivot_row
        right = right - factor * right[step : step + 1, :]
    return eye - ridge * right


def pick(count, size, at, flip):
    shape = (size, count) if flip else (count, size)
    down = lax.broadcasted_iota(jnp.int32, shape, 0)
    along = lax.broadcasted_iota(jnp.int32, shape, 1)
    gap = down - along if flip else along - down
    return jnp.where(gap == at, 1.0, 0.0).astype(jnp.bfloat16)


def windows(planes, a, b, length):
    size = planes.shape[1]
    lanes = pick(length, size, b, True)
    narrow = jnp.dot(planes.reshape(2 * size, size), lanes, preferred_element_type=jnp.float32)
    narrow = narrow.astype(jnp.bfloat16)
    both = jnp.concatenate([narrow[:size], narrow[size:]], 1)
    both = jnp.dot(pick(length, size, a, False), both, preferred_element_type=jnp.float32)
    return both[:, :length], both[:, length:]


def kernel(
    n, m, led_total,
    spectra_ref, pupils_ref, amps_ref, offsets_ref, positions_ref, first_ref, second_ref,
    out_ref,
    stack, wide, grad, from_left, from_right, peaks, places, gathered,
    peak_send, peak_recv, place_send, place_recv,
    right_send, right_recv, left_send, left_recv, tile_send, tile_recv,
):
    tl, leds = amps_ref.shape[0], amps_ref.shape[1]
    length = pupils_ref.shape[2]
    rows = length // n
    z = lax.axis_index("led")
    me = lax.axis_index("tile")
    tiles = tl * m

    def led_peer(d):
        return {"led": lax.rem(z + d, n)}

    def tile_peer(d):
        return {"tile": lax.rem(me + d, m)}

    def strip(q):
        return pl.ds(pl.multiple_of(q * rows, rows), rows)

    barrier = pltpu.get_barrier_semaphore()
    for d in range(1, n):
        pl.semaphore_signal(barrier, inc=1, device_id=led_peer(d), device_id_type=MESH)
    for d in range(1, m):
        pl.semaphore_signal(barrier, inc=1, device_id=tile_peer(d), device_id_type=MESH)

    subs = lax.broadcasted_iota(jnp.int32, (8, 128), 0)

    place = jnp.zeros((8, 128), jnp.float32)
    for t in range(tl):
        for axis in range(2):
            value = positions_ref[t, axis].astype(jnp.float32)
            place = jnp.where(subs == 2 * t + axis, value, place)
    places[0] = place

    def place_copy(d):
        return pltpu.make_async_remote_copy(
            places.at[0], places.at[d], place_send.at[d], place_recv.at[d],
            device_id=tile_peer(d), device_id_type=MESH)

    def peak_copy(d):
        return pltpu.make_async_remote_copy(
            peaks.at[0], peaks.at[d], peak_send.at[d], peak_recv.at[d],
            device_id=led_peer(d), device_id_type=MESH)

    def right_copy(t, c, q):
        return pltpu.make_async_remote_copy(
            grad.at[t, c, strip(q)], from_left.at[t, c, q],
            right_send.at[t, c, q], right_recv.at[t, c, q],
            device_id=led_peer(1), device_id_type=MESH)

    def left_copy(t, c, q):
        return pltpu.make_async_remote_copy(
            grad.at[t, c, strip(q)], from_right.at[t, c, q],
            left_send.at[t, c, q], left_recv.at[t, c, q],
            device_id=led_peer(n - 1), device_id_type=MESH)

    def tile_copy(t, c, d):
        return pltpu.make_async_remote_copy(
            gathered.at[me, t, c], gathered.at[me, t, c],
            tile_send.at[t, c, d], tile_recv.at[t, c, d],
            device_id=tile_peer(d), device_id_type=MESH)

    def tile_arrival(t, c, d):
        source = lax.rem(me + m - d, m)
        return pltpu.make_async_remote_copy(
            gathered.at[me, t, c], gathered.at[source, t, c],
            tile_send.at[t, c, d], tile_recv.at[t, c, d],
            device_id=tile_peer(d), device_id_type=MESH)

    def work(t):
        peak = jnp.zeros((1, 1), jnp.float32)
        for led in range(leds):
            a = offsets_ref[t, led, 0]
            b = offsets_ref[t, led, 1]
            window_re, window_im = windows(spectra_ref[t], a, b, length)
            pupil_re, pupil_im = (pupils_ref[t, 0], pupils_ref[t, 1])
            power = window_re * window_re + window_im * window_im
            power = jnp.max(jnp.max(power, axis=0, keepdims=True), axis=1, keepdims=True)
            peak = peak + power
            stack[led, :length] = (pupil_re * window_re - pupil_im * window_im).astype(jnp.bfloat16)
            stack[led, length:] = (pupil_re * window_im + pupil_im * window_re).astype(jnp.bfloat16)
            inner = jnp.dot(first_ref[...], stack[led], preferred_element_type=jnp.float32)
            wide[led, :, :length] = inner[:length].astype(jnp.bfloat16)
            wide[led, :, length:] = inner[length:].astype(jnp.bfloat16)
            wave = jnp.dot(wide[led], second_ref[...], preferred_element_type=jnp.float32)
            wave_re, wave_im = (wave[:, :length], wave[:, length:])
            squared = jnp.maximum(wave_re * wave_re + wave_im * wave_im, FLOOR * FLOOR)
            ratio = amps_ref[t, led].astype(jnp.float32) * lax.rsqrt(squared) - 1.0
            stack[led, :length] = (wave_re * ratio).astype(jnp.bfloat16)
            stack[led, length:] = (wave_im * ratio).astype(jnp.bfloat16)
            inner = jnp.dot(second_ref[...], stack[led], preferred_element_type=jnp.float32)
            wide[led, :, :length] = inner[:length].astype(jnp.bfloat16)
            wide[led, :, length:] = inner[length:].astype(jnp.bfloat16)
            delta = jnp.dot(wide[led], first_ref[...], preferred_element_type=jnp.float32)
            delta_re, delta_im = (delta[:, :length], delta[:, length:])
            grad_re = window_re * delta_re + window_im * delta_im
            grad_im = window_re * delta_im - window_im * delta_re
            if led == 0:
                grad[t, 0] = grad_re
                grad[t, 1] = grad_im
            else:
                grad[t, 0] += grad_re
                grad[t, 1] += grad_im
        peaks[0, t] = jnp.broadcast_to(peak, (8, 128))

    pl.semaphore_wait(barrier, n - 1 + m - 1)
    for d in range(1, m):
        place_copy(d).start()

    for t in range(tl):
        work(t)

        @pl.when(z == 0)
        def _():
            for q in range(n - 1, 0, -1):
                for c in range(2):
                    right_copy(t, c, q).start()

        @pl.when(z == n - 1)
        def _():
            for q in range(n - 1):
                for c in range(2):
                    left_copy(t, c, q).start()

    for d in range(1, n):
        peak_copy(d).start()
    for d in range(1, m):
        place_copy(d).wait_recv()
    place_rows = [None] * tiles
    for d in range(m):
        for t in range(tl):
            place_rows[d * tl + t] = (places[d, 2 * t : 2 * t + 1, :], places[d, 2 * t + 1 : 2 * t + 2, :])
    mix = mixing_matrix(place_rows, tiles)
    for d in range(1, n):
        peak_copy(d).wait_recv()

    for t in range(tl):
        peak = peaks[0, t]
        for d in range(1, n):
            peak = peak + peaks[d, t]
        mean_peak = jnp.broadcast_to((peak / led_total)[:1, :1], (rows, length))
        for d in range(n - 1, 0, -1):
            for c in range(2):
                @pl.when(jnp.logical_and(z > 0, z + d < n))
                def _():
                    q = z + d
                    right_copy(t, c, q).wait_recv()
                    grad[t, c, strip(q)] += from_left[t, c, q]
                    right_copy(t, c, q).start()

                @pl.when(jnp.logical_and(z < n - 1, z - d >= 0))
                def _():
                    q = z - d
                    left_copy(t, c, q).wait_recv()
                    grad[t, c, strip(q)] += from_right[t, c, q]
                    left_copy(t, c, q).start()
        for c in range(2):
            @pl.when(z > 0)
            def _():
                right_copy(t, c, z).wait_recv()
                grad[t, c, strip(z)] += from_left[t, c, z]

            @pl.when(z < n - 1)
            def _():
                left_copy(t, c, z).wait_recv()
                grad[t, c, strip(z)] += from_right[t, c, z]

            gathered[me, t, c] = pupils_ref[t, c, strip(z)] + grad[t, c, strip(z)] / mean_peak
            for d in range(1, m):
                tile_copy(t, c, d).start()

    for t in range(tl):
        for c in range(2):
            totals = [jnp.zeros((rows, length), jnp.float32) for _ in range(tl)]
            for d in range(m):
                if d:
                    tile_arrival(t, c, d).wait_recv()
                piece = gathered[lax.rem(me + m - d, m), t, c]
                at = d * tl + t
                for own in range(tl):
                    totals[own] += jnp.broadcast_to(mix[own : own + 1, at : at + 1], (rows, length)) * piece
            for own in range(tl):
                if t == 0:
                    out_ref[own, c] = totals[own]
                else:
                    out_ref[own, c] += totals[own]

    for d in range(1, m):
        place_copy(d).wait_send()
    for d in range(1, n):
        peak_copy(d).wait_send()
    for t in range(tl):
        for c in range(2):
            for d in range(1, m):
                tile_copy(t, c, d).wait_send()
            for d in range(1, n):
                @pl.when(z + d < n)
                def _():
                    right_copy(t, c, z + d).wait_send()

                @pl.when(z - d >= 0)
                def _():
                    left_copy(t, c, z - d).wait_send()


def per_device(n, m, spectra, pupils, amplitudes, offsets, positions):
    tl, leds = amplitudes.shape[:2]
    length = pupils.shape[2]
    rows = length // n
    first, second = inverse_tables(length)
    vmem = pl.BlockSpec(memory_space=pltpu.VMEM)
    smem = pl.BlockSpec(memory_space=pltpu.SMEM)
    dma = pltpu.SemaphoreType.DMA
    strips = pltpu.VMEM((tl, 2, n, rows, length), jnp.float32)
    return pl.pallas_call(
        functools.partial(kernel, n, m, leds * n),
        out_shape=jax.ShapeDtypeStruct((tl, 2, rows, length), jnp.float32),
        in_specs=[vmem, vmem, vmem, smem, smem, vmem, vmem],
        out_specs=vmem,
        scratch_shapes=[
            pltpu.VMEM((leds, 2 * length, length), jnp.bfloat16),
            pltpu.VMEM((leds, length, 2 * length), jnp.bfloat16),
            pltpu.VMEM((tl, 2, length, length), jnp.float32),
            strips,
            strips,
            pltpu.VMEM((n, tl, 8, 128), jnp.float32),
            pltpu.VMEM((m, 8, 128), jnp.float32),
            pltpu.VMEM((m, tl, 2, rows, length), jnp.float32),
            dma((n,)), dma((n,)), dma((m,)), dma((m,)),
            dma((tl, 2, n)), dma((tl, 2, n)), dma((tl, 2, n)), dma((tl, 2, n)),
            dma((tl, 2, m)), dma((tl, 2, m)),
        ],
        compiler_params=pltpu.CompilerParams(
            collective_id=0, has_side_effects=True, vmem_limit_bytes=40 << 20
        ),
    )(spectra, pupils, amplitudes, offsets, positions, jnp.asarray(first), jnp.asarray(second))


def solution(mesh):
    placed = (
        P(("groups", "tile"), None, None, None),
        P(("groups", "tile"), None, None, None),
        P(("groups", "tile"), "led", None, None),
        P(("groups", "tile"), "led", None),
        P(("groups", "tile"), None),
    )
    return jax.shard_map(
        functools.partial(per_device, mesh.shape["led"], mesh.shape["tile"]),
        mesh=mesh,
        in_specs=placed,
        out_specs=P(("groups", "tile"), None, "led", None),
        check_vma=False,
    )
```

```python
import functools
import math

import jax
import jax.numpy as jnp
import numpy as np
from jax import lax
from jax.experimental import pallas as pl
from jax.experimental.pallas import tpu as pltpu
from jax.sharding import PartitionSpec as P

DEG = 5
FIELD = 2048
RIDGE = 0.05
FLOOR = 0.25
MESH = pl.DeviceIdType.MESH


def inverse_tables(length):
    index = np.arange(length, dtype=np.int64)
    angle = (index[:, None] * index[None, :] % length) * (2.0 * math.pi / length)
    factor = 1.0 / math.sqrt(length)
    real_part = (np.cos(angle) * factor).astype(np.float32)
    imag_part = (np.sin(angle) * factor).astype(np.float32)
    first = np.block([[real_part, -imag_part], [imag_part, real_part]])
    second = np.block([[real_part, imag_part], [-imag_part, real_part]])
    return first.astype(jnp.bfloat16), second.astype(jnp.bfloat16)


def legendre(values):
    polys = [jnp.ones_like(values), values]
    for degree in range(2, DEG + 1):
        polys.append(((2 * degree - 1) * values * polys[-1] - (degree - 1) * polys[-2]) / degree)
    return polys


def mixing_matrix(place_rows, tiles):
    lanes = lax.broadcasted_iota(jnp.int32, (tiles, 128), 1)
    subs = lax.broadcasted_iota(jnp.int32, (tiles, 128), 0)
    ridge = RIDGE * tiles
    products = []
    for axis in range(2):
        down = jnp.zeros((tiles, 128), jnp.float32)
        along = jnp.zeros((tiles, 128), jnp.float32)
        for tile in range(tiles):
            row = jnp.broadcast_to(place_rows[tile][axis], (tiles, 128))
            down = jnp.where(subs == tile, row, down)
            along = jnp.where(lanes == tile, row, along)
        scale = 2.0 / (FIELD - 1)
        down, along = (down * scale - 1.0, along * scale - 1.0)
        products.append([a * b for a, b in zip(legendre(down), legendre(along))])
    kernel = jnp.zeros((tiles, 128), jnp.float32)
    partial = jnp.zeros((tiles, 128), jnp.float32)
    for degree in range(DEG + 1):
        partial = partial + products[1][degree]
        kernel = kernel + products[0][DEG - degree] * partial
    eye = jnp.where(subs == lanes, 1.0, 0.0)
    left = kernel + ridge * eye
    right = eye
    for step in range(tiles):
        pivot_row = left[step : step + 1, :]
        pivot = jnp.sum(jnp.where(lanes[:1] == step, pivot_row, 0.0), axis=1, keepdims=True)
        column = jnp.sum(jnp.where(lanes == step, left, 0.0), axis=1, keepdims=True)
        factor = jnp.where(subs[:, :1] == step, 1.0 - 1.0 / pivot, column / pivot)
        left = left - factor * pivot_row
        right = right - factor * right[step : step + 1, :]
    return eye - ridge * right


def pick(count, size, at, flip):
    shape = (size, count) if flip else (count, size)
    down = lax.broadcasted_iota(jnp.int32, shape, 0)
    along = lax.broadcasted_iota(jnp.int32, shape, 1)
    gap = down - along if flip else along - down
    return jnp.where(gap == at, 1.0, 0.0).astype(jnp.bfloat16)


def windows(planes, a, b, length):
    size = planes.shape[1]
    lanes = pick(length, size, b, True)
    narrow = jnp.dot(planes.reshape(2 * size, size), lanes, preferred_element_type=jnp.float32)
    narrow = narrow.astype(jnp.bfloat16)
    both = jnp.concatenate([narrow[:size], narrow[size:]], 1)
    both = jnp.dot(pick(length, size, a, False), both, preferred_element_type=jnp.float32)
    return both[:, :length], both[:, length:]


def kernel(
    n, m, led_total,
    spectra_hbm, pupils_hbm, amps_hbm, offsets_hbm, positions_hbm, first_hbm, second_hbm,
    out_ref,
    spectra_ref, pupils_ref, amps_ref, offsets_ref, positions_ref, first_ref, second_ref, load_sem,
    stack, wide, grad, from_left, from_right, peaks, places, gathered,
    peak_send, peak_recv, place_send, place_recv,
    right_send, right_recv, left_send, left_recv, tile_send, tile_recv,
):
    tl, leds = amps_ref.shape[0], amps_ref.shape[1]
    length = pupils_ref.shape[2]
    rows = length // n
    z = lax.axis_index("led")
    me = lax.axis_index("tile")
    tiles = tl * m

    def led_peer(d):
        return {"led": lax.rem(z + d, n)}

    def tile_peer(d):
        return {"tile": lax.rem(me + d, m)}

    def strip(q):
        return pl.ds(pl.multiple_of(q * rows, rows), rows)

    loads = {}
    for name, source, target in [
        ("offsets", offsets_hbm, offsets_ref),
        *[(("spectra", t), spectra_hbm.at[t], spectra_ref.at[t]) for t in range(1)],
        *[(("pupils", t), pupils_hbm.at[t], pupils_ref.at[t]) for t in range(1)],
        ("first", first_hbm, first_ref),
        ("second", second_hbm, second_ref),
        *[(("amps", t), amps_hbm.at[t], amps_ref.at[t]) for t in range(1)],
        ("positions", positions_hbm, positions_ref),
        *[(("spectra", t), spectra_hbm.at[t], spectra_ref.at[t]) for t in range(1, tl)],
        *[(("pupils", t), pupils_hbm.at[t], pupils_ref.at[t]) for t in range(1, tl)],
        *[(("amps", t), amps_hbm.at[t], amps_ref.at[t]) for t in range(1, tl)],
    ]:
        loads[name] = pltpu.make_async_copy(source, target, load_sem.at[len(loads)])
        loads[name].start()

    barrier = pltpu.get_barrier_semaphore()
    for d in range(1, n):
        pl.semaphore_signal(barrier, inc=1, device_id=led_peer(d), device_id_type=MESH)
    for d in range(1, m):
        pl.semaphore_signal(barrier, inc=1, device_id=tile_peer(d), device_id_type=MESH)

    subs = lax.broadcasted_iota(jnp.int32, (8, 128), 0)

    def place_copy(d):
        return pltpu.make_async_remote_copy(
            places.at[0], places.at[d], place_send.at[d], place_recv.at[d],
            device_id=tile_peer(d), device_id_type=MESH)

    def peak_copy(d):
        return pltpu.make_async_remote_copy(
            peaks.at[0], peaks.at[d], peak_send.at[d], peak_recv.at[d],
            device_id=led_peer(d), device_id_type=MESH)

    def right_copy(t, c, q):
        return pltpu.make_async_remote_copy(
            grad.at[t, c, strip(q)], from_left.at[t, c, q],
            right_send.at[t, c, q], right_recv.at[t, c, q],
            device_id=led_peer(1), device_id_type=MESH)

    def left_copy(t, c, q):
        return pltpu.make_async_remote_copy(
            grad.at[t, c, strip(q)], from_right.at[t, c, q],
            left_send.at[t, c, q], left_recv.at[t, c, q],
            device_id=led_peer(n - 1), device_id_type=MESH)

    def tile_copy(t, c, d):
        return pltpu.make_async_remote_copy(
            gathered.at[me, t, c], gathered.at[me, t, c],
            tile_send.at[t, c, d], tile_recv.at[t, c, d],
            device_id=tile_peer(d), device_id_type=MESH)

    def tile_arrival(t, c, d):
        source = lax.rem(me + m - d, m)
        return pltpu.make_async_remote_copy(
            gathered.at[me, t, c], gathered.at[source, t, c],
            tile_send.at[t, c, d], tile_recv.at[t, c, d],
            device_id=tile_peer(d), device_id_type=MESH)

    def work(t):
        loads["spectra", t].wait()
        if t == 0:
            loads["offsets"].wait()
        peak = jnp.zeros((1, 1), jnp.float32)
        for led in range(leds):
            a = offsets_ref[t, led, 0]
            b = offsets_ref[t, led, 1]
            window_re, window_im = windows(spectra_ref[t], a, b, length)
            if led == 0:
                loads["pupils", t].wait()
            pupil_re, pupil_im = (pupils_ref[t, 0], pupils_ref[t, 1])
            power = window_re * window_re + window_im * window_im
            power = jnp.max(jnp.max(power, axis=0, keepdims=True), axis=1, keepdims=True)
            peak = peak + power
            stack[led, :length] = (pupil_re * window_re - pupil_im * window_im).astype(jnp.bfloat16)
            stack[led, length:] = (pupil_re * window_im + pupil_im * window_re).astype(jnp.bfloat16)
            if t == 0 and led == 0:
                loads["first"].wait()
            inner = jnp.dot(first_ref[...], stack[led], preferred_element_type=jnp.float32)
            wide[led, :, :length] = inner[:length].astype(jnp.bfloat16)
            wide[led, :, length:] = inner[length:].astype(jnp.bfloat16)
            if t == 0 and led == 0:
                loads["second"].wait()
            wave = jnp.dot(wide[led], second_ref[...], preferred_element_type=jnp.float32)
            wave_re, wave_im = (wave[:, :length], wave[:, length:])
            squared = jnp.maximum(wave_re * wave_re + wave_im * wave_im, FLOOR * FLOOR)
            if led == 0:
                loads["amps", t].wait()
            ratio = amps_ref[t, led].astype(jnp.float32) * lax.rsqrt(squared) - 1.0
            stack[led, :length] = (wave_re * ratio).astype(jnp.bfloat16)
            stack[led, length:] = (wave_im * ratio).astype(jnp.bfloat16)
            inner = jnp.dot(second_ref[...], stack[led], preferred_element_type=jnp.float32)
            wide[led, :, :length] = inner[:length].astype(jnp.bfloat16)
            wide[led, :, length:] = inner[length:].astype(jnp.bfloat16)
            delta = jnp.dot(wide[led], first_ref[...], preferred_element_type=jnp.float32)
            delta_re, delta_im = (delta[:, :length], delta[:, length:])
            grad_re = window_re * delta_re + window_im * delta_im
            grad_im = window_re * delta_im - window_im * delta_re
            if led == 0:
                grad[t, 0] = grad_re
                grad[t, 1] = grad_im
            else:
                grad[t, 0] += grad_re
                grad[t, 1] += grad_im
        peaks[0, t] = jnp.broadcast_to(peak, (8, 128))


    for t in range(tl):
        work(t)
        if t == 0:
            pl.semaphore_wait(barrier, n - 1 + m - 1)

        @pl.when(z == 0)
        def _():
            for q in range(n - 1, 0, -1):
                for c in range(2):
                    right_copy(t, c, q).start()

        @pl.when(z == n - 1)
        def _():
            for q in range(n - 1):
                for c in range(2):
                    left_copy(t, c, q).start()

    for d in range(1, n):
        peak_copy(d).start()
    loads["positions"].wait()
    place = jnp.zeros((8, 128), jnp.float32)
    for t in range(tl):
        for axis in range(2):
            value = positions_ref[t, axis].astype(jnp.float32)
            place = jnp.where(subs == 2 * t + axis, value, place)
    places[0] = place

    for d in range(1, m):
        place_copy(d).start()
    for d in range(1, m):
        place_copy(d).wait_recv()
    place_rows = [None] * tiles
    for d in range(m):
        for t in range(tl):
            place_rows[d * tl + t] = (places[d, 2 * t : 2 * t + 1, :], places[d, 2 * t + 1 : 2 * t + 2, :])
    mix = mixing_matrix(place_rows, tiles)
    for d in range(1, n):
        peak_copy(d).wait_recv()

    for t in range(tl):
        peak = peaks[0, t]
        for d in range(1, n):
            peak = peak + peaks[d, t]
        mean_peak = jnp.broadcast_to((peak / led_total)[:1, :1], (rows, length))
        for d in range(n - 1, 0, -1):
            for c in range(2):
                @pl.when(jnp.logical_and(z > 0, z + d < n))
                def _():
                    q = z + d
                    right_copy(t, c, q).wait_recv()
                    grad[t, c, strip(q)] += from_left[t, c, q]
                    right_copy(t, c, q).start()

                @pl.when(jnp.logical_and(z < n - 1, z - d >= 0))
                def _():
                    q = z - d
                    left_copy(t, c, q).wait_recv()
                    grad[t, c, strip(q)] += from_right[t, c, q]
                    left_copy(t, c, q).start()
        for c in range(2):
            @pl.when(z > 0)
            def _():
                right_copy(t, c, z).wait_recv()
                grad[t, c, strip(z)] += from_left[t, c, z]

            @pl.when(z < n - 1)
            def _():
                left_copy(t, c, z).wait_recv()
                grad[t, c, strip(z)] += from_right[t, c, z]

            gathered[me, t, c] = pupils_ref[t, c, strip(z)] + grad[t, c, strip(z)] / mean_peak
            for d in range(1, m):
                tile_copy(t, c, d).start()

    for t in range(tl):
        for c in range(2):
            totals = [jnp.zeros((rows, length), jnp.float32) for _ in range(tl)]
            for d in range(m):
                if d:
                    tile_arrival(t, c, d).wait_recv()
                piece = gathered[lax.rem(me + m - d, m), t, c]
                at = d * tl + t
                for own in range(tl):
                    totals[own] += jnp.broadcast_to(mix[own : own + 1, at : at + 1], (rows, length)) * piece
            for own in range(tl):
                if t == 0:
                    out_ref[own, c] = totals[own]
                else:
                    out_ref[own, c] += totals[own]

    for d in range(1, m):
        place_copy(d).wait_send()
    for d in range(1, n):
        peak_copy(d).wait_send()
    for t in range(tl):
        for c in range(2):
            for d in range(1, m):
                tile_copy(t, c, d).wait_send()
            for d in range(1, n):
                @pl.when(z + d < n)
                def _():
                    right_copy(t, c, z + d).wait_send()

                @pl.when(z - d >= 0)
                def _():
                    left_copy(t, c, z - d).wait_send()


def per_device(n, m, spectra, pupils, amplitudes, offsets, positions):
    tl, leds = amplitudes.shape[:2]
    length = pupils.shape[2]
    rows = length // n
    vmem = pl.BlockSpec(memory_space=pltpu.VMEM)
    hbm = pl.BlockSpec(memory_space=pltpu.HBM)
    first, second = (jnp.asarray(table) for table in inverse_tables(length))
    operands = (spectra, pupils, amplitudes, offsets, positions, first, second)
    dma = pltpu.SemaphoreType.DMA
    strips = pltpu.VMEM((tl, 2, n, rows, length), jnp.float32)
    return pl.pallas_call(
        functools.partial(kernel, n, m, leds * n),
        out_shape=jax.ShapeDtypeStruct((tl, 2, rows, length), jnp.float32),
        in_specs=[hbm] * 7,
        out_specs=vmem,
        scratch_shapes=[
            *[
                (pltpu.SMEM if each.dtype == jnp.int32 else pltpu.VMEM)(each.shape, each.dtype)
                for each in operands
            ],
            dma((4 + 3 * tl,)),
            pltpu.VMEM((leds, 2 * length, length), jnp.bfloat16),
            pltpu.VMEM((leds, length, 2 * length), jnp.bfloat16),
            pltpu.VMEM((tl, 2, length, length), jnp.float32),
            strips,
            strips,
            pltpu.VMEM((n, tl, 8, 128), jnp.float32),
            pltpu.VMEM((m, 8, 128), jnp.float32),
            pltpu.VMEM((m, tl, 2, rows, length), jnp.float32),
            dma((n,)), dma((n,)), dma((m,)), dma((m,)),
            dma((tl, 2, n)), dma((tl, 2, n)), dma((tl, 2, n)), dma((tl, 2, n)),
            dma((tl, 2, m)), dma((tl, 2, m)),
        ],
        compiler_params=pltpu.CompilerParams(
            collective_id=0, has_side_effects=True, vmem_limit_bytes=40 << 20
        ),
    )(*operands)


def solution(mesh):
    placed = (
        P(("groups", "tile"), None, None, None),
        P(("groups", "tile"), None, None, None),
        P(("groups", "tile"), "led", None, None),
        P(("groups", "tile"), "led", None),
        P(("groups", "tile"), None),
    )
    return jax.shard_map(
        functools.partial(per_device, mesh.shape["led"], mesh.shape["tile"]),
        mesh=mesh,
        in_specs=placed,
        out_specs=P(("groups", "tile"), None, "led", None),
        check_vma=False,
    )
```

```python
import functools
import math

import jax
import jax.numpy as jnp
import numpy as np
from jax import lax
from jax.experimental import pallas as pl
from jax.experimental.pallas import tpu as pltpu
from jax.sharding import PartitionSpec as P

DEG = 5
FIELD = 2048
RIDGE = 0.05
FLOOR = 0.25
MESH = pl.DeviceIdType.MESH
FLIGHT = 3


def inverse_tables(length):
    index = np.arange(length, dtype=np.int64)
    angle = (index[:, None] * index[None, :] % length) * (2.0 * math.pi / length)
    factor = 1.0 / math.sqrt(length)
    real_part = (np.cos(angle) * factor).astype(np.float32)
    imag_part = (np.sin(angle) * factor).astype(np.float32)
    first = np.block([[real_part, -imag_part], [imag_part, real_part]])
    second = np.block([[real_part, imag_part], [-imag_part, real_part]])
    return first.astype(jnp.bfloat16), second.astype(jnp.bfloat16)


def legendre(values):
    polys = [jnp.ones_like(values), values]
    for degree in range(2, DEG + 1):
        polys.append(((2 * degree - 1) * values * polys[-1] - (degree - 1) * polys[-2]) / degree)
    return polys


def mixing_matrix(place_rows, tiles):
    lanes = lax.broadcasted_iota(jnp.int32, (tiles, 128), 1)
    subs = lax.broadcasted_iota(jnp.int32, (tiles, 128), 0)
    ridge = RIDGE * tiles
    products = []
    for axis in range(2):
        down = jnp.zeros((tiles, 128), jnp.float32)
        along = jnp.zeros((tiles, 128), jnp.float32)
        for tile in range(tiles):
            row = jnp.broadcast_to(place_rows[tile][axis], (tiles, 128))
            down = jnp.where(subs == tile, row, down)
            along = jnp.where(lanes == tile, row, along)
        scale = 2.0 / (FIELD - 1)
        down, along = (down * scale - 1.0, along * scale - 1.0)
        products.append([a * b for a, b in zip(legendre(down), legendre(along))])
    kernel = jnp.zeros((tiles, 128), jnp.float32)
    partial = jnp.zeros((tiles, 128), jnp.float32)
    for degree in range(DEG + 1):
        partial = partial + products[1][degree]
        kernel = kernel + products[0][DEG - degree] * partial
    eye = jnp.where(subs == lanes, 1.0, 0.0)
    left = kernel + ridge * eye
    right = eye
    for step in range(tiles):
        pivot_row = left[step : step + 1, :]
        pivot = jnp.sum(jnp.where(lanes[:1] == step, pivot_row, 0.0), axis=1, keepdims=True)
        column = jnp.sum(jnp.where(lanes == step, left, 0.0), axis=1, keepdims=True)
        factor = jnp.where(subs[:, :1] == step, 1.0 - 1.0 / pivot, column / pivot)
        left = left - factor * pivot_row
        right = right - factor * right[step : step + 1, :]
    return eye - ridge * right


def pick(count, size, at, flip):
    shape = (size, count) if flip else (count, size)
    down = lax.broadcasted_iota(jnp.int32, shape, 0)
    along = lax.broadcasted_iota(jnp.int32, shape, 1)
    gap = down - along if flip else along - down
    return jnp.where(gap == at, 1.0, 0.0).astype(jnp.bfloat16)


def windows(planes, a, b, length):
    size = planes.shape[1]
    lanes = pick(length, size, b, True)
    narrow = jnp.dot(planes.reshape(2 * size, size), lanes, preferred_element_type=jnp.float32)
    narrow = narrow.astype(jnp.bfloat16)
    both = jnp.concatenate([narrow[:size], narrow[size:]], 1)
    both = jnp.dot(pick(length, size, a, False), both, preferred_element_type=jnp.float32)
    return both[:, :length], both[:, length:]


def kernel(
    n, m, led_total,
    spectra_hbm, pupils_hbm, amps_hbm, offsets_hbm, positions_hbm, first_hbm, second_hbm,
    out_ref,
    spectra_ref, pupils_ref, amps_ref, offsets_ref, positions_ref, first_ref, second_ref, load_sem,
    stack, wide, grad, from_left, from_right, peaks, places, gathered,
    peak_send, peak_recv, place_send, place_recv,
    right_send, right_recv, left_send, left_recv, tile_send, tile_recv,
):
    tl, leds = amps_ref.shape[0], amps_ref.shape[1]
    length = pupils_ref.shape[2]
    rows = length // n
    z = lax.axis_index("led")
    me = lax.axis_index("tile")
    tiles = tl * m

    def led_peer(d):
        return {"led": lax.rem(z + d, n)}

    def tile_peer(d):
        return {"tile": lax.rem(me + d, m)}

    def strip(q):
        return pl.ds(pl.multiple_of(q * rows, rows), rows)

    loads = {}
    for name, source, target in [
        ("offsets", offsets_hbm, offsets_ref),
        *[(("spectra", t), spectra_hbm.at[t], spectra_ref.at[t]) for t in range(1)],
        *[(("pupils", t), pupils_hbm.at[t], pupils_ref.at[t]) for t in range(1)],
        ("first", first_hbm, first_ref),
        ("second", second_hbm, second_ref),
        *[(("amps", t), amps_hbm.at[t], amps_ref.at[t]) for t in range(1)],
        ("positions", positions_hbm, positions_ref),
        *[(("spectra", t), spectra_hbm.at[t], spectra_ref.at[t]) for t in range(1, tl)],
        *[(("pupils", t), pupils_hbm.at[t], pupils_ref.at[t]) for t in range(1, tl)],
        *[(("amps", t), amps_hbm.at[t], amps_ref.at[t]) for t in range(1, tl)],
    ]:
        loads[name] = pltpu.make_async_copy(source, target, load_sem.at[len(loads)])
        loads[name].start()

    barrier = pltpu.get_barrier_semaphore()
    for d in range(1, n):
        pl.semaphore_signal(barrier, inc=1, device_id=led_peer(d), device_id_type=MESH)
    for d in range(1, m):
        pl.semaphore_signal(barrier, inc=1, device_id=tile_peer(d), device_id_type=MESH)

    subs = lax.broadcasted_iota(jnp.int32, (8, 128), 0)

    def place_copy(d):
        return pltpu.make_async_remote_copy(
            places.at[0], places.at[d], place_send.at[d], place_recv.at[d],
            device_id=tile_peer(d), device_id_type=MESH)

    def peak_copy(d):
        return pltpu.make_async_remote_copy(
            peaks.at[0], peaks.at[d], peak_send.at[d], peak_recv.at[d],
            device_id=led_peer(d), device_id_type=MESH)

    def right_copy(t, c, q):
        return pltpu.make_async_remote_copy(
            grad.at[t, c, strip(q)], from_left.at[t, c, q],
            right_send.at[t, c, q], right_recv.at[t, c, q],
            device_id=led_peer(1), device_id_type=MESH)

    def left_copy(t, c, q):
        return pltpu.make_async_remote_copy(
            grad.at[t, c, strip(q)], from_right.at[t, c, q],
            left_send.at[t, c, q], left_recv.at[t, c, q],
            device_id=led_peer(n - 1), device_id_type=MESH)

    def tile_copy(t, c, d):
        return pltpu.make_async_remote_copy(
            gathered.at[me, t, c], gathered.at[me, t, c],
            tile_send.at[t, c, d], tile_recv.at[t, c, d],
            device_id=tile_peer(d), device_id_type=MESH)

    def tile_arrival(t, c, d):
        source = lax.rem(me + m - d, m)
        return pltpu.make_async_remote_copy(
            gathered.at[me, t, c], gathered.at[source, t, c],
            tile_send.at[t, c, d], tile_recv.at[t, c, d],
            device_id=tile_peer(d), device_id_type=MESH)

    def work(t):
        loads["spectra", t].wait()
        if t == 0:
            loads["offsets"].wait()
        peak = jnp.zeros((1, 1), jnp.float32)
        for led in range(leds):
            a = offsets_ref[t, led, 0]
            b = offsets_ref[t, led, 1]
            window_re, window_im = windows(spectra_ref[t], a, b, length)
            if led == 0:
                loads["pupils", t].wait()
            pupil_re, pupil_im = (pupils_ref[t, 0], pupils_ref[t, 1])
            power = window_re * window_re + window_im * window_im
            power = jnp.max(jnp.max(power, axis=0, keepdims=True), axis=1, keepdims=True)
            peak = peak + power
            stack[led, :length] = (pupil_re * window_re - pupil_im * window_im).astype(jnp.bfloat16)
            stack[led, length:] = (pupil_re * window_im + pupil_im * window_re).astype(jnp.bfloat16)
            if t == 0 and led == 0:
                loads["first"].wait()
            inner = jnp.dot(first_ref[...], stack[led], preferred_element_type=jnp.float32)
            wide[led, :, :length] = inner[:length].astype(jnp.bfloat16)
            wide[led, :, length:] = inner[length:].astype(jnp.bfloat16)
            if t == 0 and led == 0:
                loads["second"].wait()
            wave = jnp.dot(wide[led], second_ref[...], preferred_element_type=jnp.float32)
            wave_re, wave_im = (wave[:, :length], wave[:, length:])
            squared = jnp.maximum(wave_re * wave_re + wave_im * wave_im, FLOOR * FLOOR)
            if led == 0:
                loads["amps", t].wait()
            ratio = amps_ref[t, led].astype(jnp.float32) * lax.rsqrt(squared) - 1.0
            stack[led, :length] = (wave_re * ratio).astype(jnp.bfloat16)
            stack[led, length:] = (wave_im * ratio).astype(jnp.bfloat16)
            inner = jnp.dot(second_ref[...], stack[led], preferred_element_type=jnp.float32)
            wide[led, :, :length] = inner[:length].astype(jnp.bfloat16)
            wide[led, :, length:] = inner[length:].astype(jnp.bfloat16)
            delta = jnp.dot(wide[led], first_ref[...], preferred_element_type=jnp.float32)
            delta_re, delta_im = (delta[:, :length], delta[:, length:])
            grad_re = window_re * delta_re + window_im * delta_im
            grad_im = window_re * delta_im - window_im * delta_re
            if led == 0:
                grad[t, 0] = grad_re
                grad[t, 1] = grad_im
            else:
                grad[t, 0] += grad_re
                grad[t, 1] += grad_im
        peaks[0, t] = jnp.broadcast_to(peak, (8, 128))


    def mixed_rows():
        for d in range(1, m):
            place_copy(d).wait_recv()
        place_rows = [
            (places[d, 2 * t : 2 * t + 1, :], places[d, 2 * t + 1 : 2 * t + 2, :])
            for d in range(m)
            for t in range(tl)
        ]
        return mixing_matrix(place_rows, tiles)

    per_tile = 2 * (n - 1)

    def end_copy(k, side):
        t, rest = divmod(k, per_tile)
        d, c = n - 1 - rest // 2, rest % 2
        return right_copy(t, c, d) if side == 0 else left_copy(t, c, n - 1 - d)

    def push(k):
        for side, end in ((0, 0), (1, n - 1)):
            @pl.when(z == end)
            def _():
                if k >= FLIGHT:
                    end_copy(k - FLIGHT, side).wait_send()
                end_copy(k, side).start()

    early = min(FLIGHT, per_tile)
    work(0)
    pl.semaphore_wait(barrier, n - 1 + m - 1)
    for k in range(early):
        push(k)
    loads["positions"].wait()
    place = jnp.zeros((8, 128), jnp.float32)
    for t in range(tl):
        for axis in range(2):
            value = positions_ref[t, axis].astype(jnp.float32)
            place = jnp.where(subs == 2 * t + axis, value, place)
    places[0] = place

    for d in range(1, m):
        place_copy(d).start()
    for t in range(1, tl):
        work(t)
    for d in range(1, n):
        peak_copy(d).start()

    for t in range(tl):
        for k in range(early if t == 0 else t * per_tile, (t + 1) * per_tile):
            push(k)
        for d in range(n - 1, 0, -1):
            for c in range(2):
                @pl.when(jnp.logical_and(z > 0, z + d < n))
                def _():
                    q = z + d
                    right_copy(t, c, q).wait_recv()
                    grad[t, c, strip(q)] += from_left[t, c, q]
                    right_copy(t, c, q).start()

                @pl.when(jnp.logical_and(z < n - 1, z - d >= 0))
                def _():
                    q = z - d
                    left_copy(t, c, q).wait_recv()
                    grad[t, c, strip(q)] += from_right[t, c, q]
                    left_copy(t, c, q).start()
        if t == 0:
            for d in range(1, n):
                peak_copy(d).wait_recv()
        peak = peaks[0, t]
        for d in range(1, n):
            peak = peak + peaks[d, t]
        mean_peak = jnp.broadcast_to((peak / led_total)[:1, :1], (rows, length))
        for c in range(2):
            @pl.when(z > 0)
            def _():
                right_copy(t, c, z).wait_recv()
                grad[t, c, strip(z)] += from_left[t, c, z]

            @pl.when(z < n - 1)
            def _():
                left_copy(t, c, z).wait_recv()
                grad[t, c, strip(z)] += from_right[t, c, z]

            gathered[me, t, c] = pupils_ref[t, c, strip(z)] + grad[t, c, strip(z)] / mean_peak
            for d in range(1, m):
                tile_copy(t, c, d).start()
        if t == 0:
            mix = mixed_rows()

    for t in range(tl):
        for c in range(2):
            totals = [jnp.zeros((rows, length), jnp.float32) for _ in range(tl)]
            for d in range(m):
                if d:
                    tile_arrival(t, c, d).wait_recv()
                piece = gathered[lax.rem(me + m - d, m), t, c]
                at = d * tl + t
                for own in range(tl):
                    totals[own] += jnp.broadcast_to(mix[own : own + 1, at : at + 1], (rows, length)) * piece
            for own in range(tl):
                if t == 0:
                    out_ref[own, c] = totals[own]
                else:
                    out_ref[own, c] += totals[own]

    for d in range(1, m):
        place_copy(d).wait_send()
    for d in range(1, n):
        peak_copy(d).wait_send()
    for t in range(tl):
        for c in range(2):
            for d in range(1, m):
                tile_copy(t, c, d).wait_send()
            for d in range(1, n):
                @pl.when(jnp.logical_and(z > 0, z + d < n))
                def _():
                    right_copy(t, c, z + d).wait_send()

                @pl.when(jnp.logical_and(z < n - 1, z - d >= 0))
                def _():
                    left_copy(t, c, z - d).wait_send()
    for k in range(max(tl * per_tile - FLIGHT, 0), tl * per_tile):
        for side, end in ((0, 0), (1, n - 1)):
            @pl.when(z == end)
            def _():
                end_copy(k, side).wait_send()


def per_device(n, m, spectra, pupils, amplitudes, offsets, positions):
    tl, leds = amplitudes.shape[:2]
    length = pupils.shape[2]
    rows = length // n
    vmem = pl.BlockSpec(memory_space=pltpu.VMEM)
    hbm = pl.BlockSpec(memory_space=pltpu.HBM)
    first, second = (jnp.asarray(table) for table in inverse_tables(length))
    operands = (spectra, pupils, amplitudes, offsets, positions, first, second)
    dma = pltpu.SemaphoreType.DMA
    strips = pltpu.VMEM((tl, 2, n, rows, length), jnp.float32)
    return pl.pallas_call(
        functools.partial(kernel, n, m, leds * n),
        out_shape=jax.ShapeDtypeStruct((tl, 2, rows, length), jnp.float32),
        in_specs=[hbm] * 7,
        out_specs=vmem,
        scratch_shapes=[
            *[
                (pltpu.SMEM if each.dtype == jnp.int32 else pltpu.VMEM)(each.shape, each.dtype)
                for each in operands
            ],
            dma((4 + 3 * tl,)),
            pltpu.VMEM((leds, 2 * length, length), jnp.bfloat16),
            pltpu.VMEM((leds, length, 2 * length), jnp.bfloat16),
            pltpu.VMEM((tl, 2, length, length), jnp.float32),
            strips,
            strips,
            pltpu.VMEM((n, tl, 8, 128), jnp.float32),
            pltpu.VMEM((m, 8, 128), jnp.float32),
            pltpu.VMEM((m, tl, 2, rows, length), jnp.float32),
            dma((n,)), dma((n,)), dma((m,)), dma((m,)),
            dma((tl, 2, n)), dma((tl, 2, n)), dma((tl, 2, n)), dma((tl, 2, n)),
            dma((tl, 2, m)), dma((tl, 2, m)),
        ],
        compiler_params=pltpu.CompilerParams(
            collective_id=0, has_side_effects=True, vmem_limit_bytes=60 << 20
        ),
    )(*operands)


def solution(mesh):
    placed = (
        P(("groups", "tile"), None, None, None),
        P(("groups", "tile"), None, None, None),
        P(("groups", "tile"), "led", None, None),
        P(("groups", "tile"), "led", None),
        P(("groups", "tile"), None),
    )
    return jax.shard_map(
        functools.partial(per_device, mesh.shape["led"], mesh.shape["tile"]),
        mesh=mesh,
        in_specs=placed,
        out_specs=P(("groups", "tile"), None, "led", None),
        check_vma=False,
    )
```

```python
import functools
import math

import jax
import jax.numpy as jnp
import numpy as np
from jax import lax
from jax.experimental import pallas as pl
from jax.experimental.pallas import tpu as pltpu
from jax.sharding import PartitionSpec as P

DEG = 5
FIELD = 2048
RIDGE = 0.05
FLOOR = 0.25
MESH = pl.DeviceIdType.MESH
FLIGHT = 4
EARLY = 4
AHEAD = 3


def inverse_tables(length):
    index = np.arange(length, dtype=np.int64)
    angle = (index[:, None] * index[None, :] % length) * (2.0 * math.pi / length)
    factor = 1.0 / math.sqrt(length)
    real_part = (np.cos(angle) * factor).astype(np.float32)
    imag_part = (np.sin(angle) * factor).astype(np.float32)
    first = np.block([[real_part, -imag_part], [imag_part, real_part]])
    second = np.block([[real_part, imag_part], [-imag_part, real_part]])
    return first.astype(jnp.bfloat16), second.astype(jnp.bfloat16)


def legendre(values):
    polys = [jnp.ones_like(values), values]
    for degree in range(2, DEG + 1):
        polys.append(((2 * degree - 1) * values * polys[-1] - (degree - 1) * polys[-2]) / degree)
    return polys


def mixing_matrix(place_rows, tiles):
    lanes = lax.broadcasted_iota(jnp.int32, (tiles, 128), 1)
    subs = lax.broadcasted_iota(jnp.int32, (tiles, 128), 0)
    ridge = RIDGE * tiles
    products = []
    for axis in range(2):
        down = jnp.zeros((tiles, 128), jnp.float32)
        along = jnp.zeros((tiles, 128), jnp.float32)
        for tile in range(tiles):
            row = jnp.broadcast_to(place_rows[tile][axis], (tiles, 128))
            down = jnp.where(subs == tile, row, down)
            along = jnp.where(lanes == tile, row, along)
        scale = 2.0 / (FIELD - 1)
        down, along = (down * scale - 1.0, along * scale - 1.0)
        products.append([a * b for a, b in zip(legendre(down), legendre(along))])
    kernel = jnp.zeros((tiles, 128), jnp.float32)
    partial = jnp.zeros((tiles, 128), jnp.float32)
    for degree in range(DEG + 1):
        partial = partial + products[1][degree]
        kernel = kernel + products[0][DEG - degree] * partial
    eye = jnp.where(subs == lanes, 1.0, 0.0)
    left = kernel + ridge * eye
    right = eye
    for step in range(tiles):
        pivot_row = left[step : step + 1, :]
        pivot = jnp.sum(jnp.where(lanes[:1] == step, pivot_row, 0.0), axis=1, keepdims=True)
        column = jnp.sum(jnp.where(lanes == step, left, 0.0), axis=1, keepdims=True)
        factor = jnp.where(subs[:, :1] == step, 1.0 - 1.0 / pivot, column / pivot)
        left = left - factor * pivot_row
        right = right - factor * right[step : step + 1, :]
    return eye - ridge * right


def pick(count, size, at, flip):
    shape = (size, count) if flip else (count, size)
    down = lax.broadcasted_iota(jnp.int32, shape, 0)
    along = lax.broadcasted_iota(jnp.int32, shape, 1)
    gap = down - along if flip else along - down
    return jnp.where(gap == at, 1.0, 0.0).astype(jnp.bfloat16)


def windows(planes, a, b, length):
    size = planes.shape[1]
    lanes = pick(length, size, b, True)
    narrow = jnp.dot(planes.reshape(2 * size, size), lanes, preferred_element_type=jnp.float32)
    narrow = narrow.astype(jnp.bfloat16)
    both = jnp.concatenate([narrow[:size], narrow[size:]], 1)
    both = jnp.dot(pick(length, size, a, False), both, preferred_element_type=jnp.float32)
    return both[:, :length], both[:, length:]


def kernel(
    n, m, led_total,
    spectra_hbm, pupils_hbm, amps_hbm, offsets_hbm, positions_hbm, first_hbm, second_hbm,
    out_ref,
    spectra_ref, pupils_ref, amps_ref, offsets_ref, positions_ref, first_ref, second_ref, load_sem,
    stack, wide, grad, from_left, from_right, peaks, places, gathered,
    peak_send, peak_recv, place_send, place_recv,
    right_send, right_recv, left_send, left_recv, tile_send, tile_recv,
):
    tl, leds = amps_ref.shape[0], amps_ref.shape[1]
    length = pupils_ref.shape[2]
    rows = length // n
    z = lax.axis_index("led")
    me = lax.axis_index("tile")
    tiles = tl * m

    def led_peer(d):
        return {"led": lax.rem(z + d, n)}

    other = me + 1 - 2 * lax.rem(me, 2)

    def tile_peer(j):
        return {"tile": lax.rem((other if j % 2 else me) + j // 2 * 2, m)}

    def tile_source(j):
        return lax.rem((other if j % 2 else me) + m - j // 2 * 2, m)

    def strip(q):
        return pl.ds(pl.multiple_of(q * rows, rows), rows)

    loads = {}
    for name, source, target in [
        ("offsets", offsets_hbm, offsets_ref),
        *[(("spectra", t), spectra_hbm.at[t], spectra_ref.at[t]) for t in range(1)],
        *[(("pupils", t), pupils_hbm.at[t], pupils_ref.at[t]) for t in range(1)],
        ("first", first_hbm, first_ref),
        ("second", second_hbm, second_ref),
        *[(("amps", t), amps_hbm.at[t], amps_ref.at[t]) for t in range(1)],
        ("positions", positions_hbm, positions_ref),
        *[(("spectra", t), spectra_hbm.at[t], spectra_ref.at[t]) for t in range(1, tl)],
        *[(("pupils", t), pupils_hbm.at[t], pupils_ref.at[t]) for t in range(1, tl)],
        *[(("amps", t), amps_hbm.at[t], amps_ref.at[t]) for t in range(1, tl)],
    ]:
        loads[name] = pltpu.make_async_copy(source, target, load_sem.at[len(loads)])
        loads[name].start()

    barrier = pltpu.get_barrier_semaphore()
    for d in range(1, n):
        pl.semaphore_signal(barrier, inc=1, device_id=led_peer(d), device_id_type=MESH)
    for d in range(1, m):
        pl.semaphore_signal(barrier, inc=1, device_id=tile_peer(d), device_id_type=MESH)

    subs = lax.broadcasted_iota(jnp.int32, (8, 128), 0)

    def place_copy(d):
        return pltpu.make_async_remote_copy(
            places.at[0], places.at[d], place_send.at[d], place_recv.at[d],
            device_id=tile_peer(d), device_id_type=MESH)

    def peak_copy(d):
        return pltpu.make_async_remote_copy(
            peaks.at[0], peaks.at[d], peak_send.at[d], peak_recv.at[d],
            device_id=led_peer(d), device_id_type=MESH)

    def right_copy(t, c, q):
        return pltpu.make_async_remote_copy(
            grad.at[t, c, strip(q)], from_left.at[t, c, q],
            right_send.at[t, c, q], right_recv.at[t, c, q],
            device_id=led_peer(1), device_id_type=MESH)

    def left_copy(t, c, q):
        return pltpu.make_async_remote_copy(
            grad.at[t, c, strip(q)], from_right.at[t, c, q],
            left_send.at[t, c, q], left_recv.at[t, c, q],
            device_id=led_peer(n - 1), device_id_type=MESH)

    def tile_copy(t, c, j):
        strip_at = gathered.at[tile_source(j - 1) if j % 2 else me, t, c]
        return pltpu.make_async_remote_copy(
            strip_at, strip_at, tile_send.at[t, c, j], tile_recv.at[t, c, j],
            device_id=tile_peer(1 if j % 2 else j), device_id_type=MESH)

    def tile_arrival(t, c, j):
        strip_at = gathered.at[tile_source(j), t, c]
        return pltpu.make_async_remote_copy(
            strip_at, strip_at, tile_send.at[t, c, j], tile_recv.at[t, c, j],
            device_id=tile_peer(j), device_id_type=MESH)

    def hand_over(t, c):
        for j in range(2, m, 2):
            tile_arrival(t, c, j).wait_recv()
            tile_copy(t, c, j + 1).start()

    def mix_in(t, c):
        totals = [jnp.zeros((rows, length), jnp.float32) for _ in range(tl)]
        for j in range(m):
            if j % 2:
                tile_arrival(t, c, j).wait_recv()
            piece = gathered[tile_source(j), t, c]
            at = j * tl + t
            for own in range(tl):
                share = jnp.broadcast_to(mix[own : own + 1, at : at + 1], (rows, length))
                totals[own] += share * piece
        for own in range(tl):
            if t == 0:
                out_ref[own, c] = totals[own]
            else:
                out_ref[own, c] += totals[own]

    def work(t):
        loads["spectra", t].wait()
        if t == 0:
            loads["offsets"].wait()
        peak = jnp.zeros((1, 1), jnp.float32)
        for led in range(leds):
            a = offsets_ref[t, led, 0]
            b = offsets_ref[t, led, 1]
            window_re, window_im = windows(spectra_ref[t], a, b, length)
            if led == 0:
                loads["pupils", t].wait()
            pupil_re, pupil_im = (pupils_ref[t, 0], pupils_ref[t, 1])
            power = window_re * window_re + window_im * window_im
            power = jnp.max(jnp.max(power, axis=0, keepdims=True), axis=1, keepdims=True)
            peak = peak + power
            stack[led, :length] = (pupil_re * window_re - pupil_im * window_im).astype(jnp.bfloat16)
            stack[led, length:] = (pupil_re * window_im + pupil_im * window_re).astype(jnp.bfloat16)
            if t == 0 and led == 0:
                loads["first"].wait()
            inner = jnp.dot(first_ref[...], stack[led], preferred_element_type=jnp.float32)
            wide[led, :, :length] = inner[:length].astype(jnp.bfloat16)
            wide[led, :, length:] = inner[length:].astype(jnp.bfloat16)
            if t == 0 and led == 0:
                loads["second"].wait()
            wave = jnp.dot(wide[led], second_ref[...], preferred_element_type=jnp.float32)
            wave_re, wave_im = (wave[:, :length], wave[:, length:])
            squared = jnp.maximum(wave_re * wave_re + wave_im * wave_im, FLOOR * FLOOR)
            if led == 0:
                loads["amps", t].wait()
            ratio = amps_ref[t, led].astype(jnp.float32) * lax.rsqrt(squared) - 1.0
            stack[led, :length] = (wave_re * ratio).astype(jnp.bfloat16)
            stack[led, length:] = (wave_im * ratio).astype(jnp.bfloat16)
            inner = jnp.dot(second_ref[...], stack[led], preferred_element_type=jnp.float32)
            wide[led, :, :length] = inner[:length].astype(jnp.bfloat16)
            wide[led, :, length:] = inner[length:].astype(jnp.bfloat16)
            delta = jnp.dot(wide[led], first_ref[...], preferred_element_type=jnp.float32)
            delta_re, delta_im = (delta[:, :length], delta[:, length:])
            grad_re = window_re * delta_re + window_im * delta_im
            grad_im = window_re * delta_im - window_im * delta_re
            if led == 0:
                grad[t, 0] = grad_re
                grad[t, 1] = grad_im
            else:
                grad[t, 0] += grad_re
                grad[t, 1] += grad_im
        peaks[0, t] = jnp.broadcast_to(peak, (8, 128))


    def mixed_rows():
        for d in range(1, m):
            place_copy(d).wait_recv()
        place_rows = [
            (places[d, 2 * t : 2 * t + 1, :], places[d, 2 * t + 1 : 2 * t + 2, :])
            for d in range(m)
            for t in range(tl)
        ]
        return mixing_matrix(place_rows, tiles)

    per_tile = 2 * (n - 1)

    def end_copy(k, side):
        t, rest = divmod(k, per_tile)
        d, c = n - 1 - rest // 2, rest % 2
        return right_copy(t, c, d) if side == 0 else left_copy(t, c, n - 1 - d)

    def push(k):
        for side, end in ((0, 0), (1, n - 1)):
            @pl.when(z == end)
            def _():
                if k >= FLIGHT:
                    end_copy(k - FLIGHT, side).wait_send()
                end_copy(k, side).start()

    work(0)
    pl.semaphore_wait(barrier, n - 1 + m - 1)
    for k in range(min(EARLY, per_tile)):
        push(k)
    loads["positions"].wait()
    place = jnp.zeros((8, 128), jnp.float32)
    for t in range(tl):
        for axis in range(2):
            value = positions_ref[t, axis].astype(jnp.float32)
            place = jnp.where(subs == 2 * t + axis, value, place)
    places[0] = place

    for d in range(1, m):
        place_copy(d).start()
    for t in range(1, tl):
        work(t)
    for d in range(1, n):
        peak_copy(d).start()
    later = min(tl * per_tile, per_tile + AHEAD)
    for k in range(min(EARLY, per_tile), later):
        push(k)

    for t in range(tl):
        for d in range(n - 1, 0, -1):
            for c in range(2):
                @pl.when(jnp.logical_and(z > 0, z + d < n))
                def _():
                    q = z + d
                    right_copy(t, c, q).wait_recv()
                    grad[t, c, strip(q)] += from_left[t, c, q]
                    right_copy(t, c, q).start()

                @pl.when(jnp.logical_and(z < n - 1, z - d >= 0))
                def _():
                    q = z - d
                    left_copy(t, c, q).wait_recv()
                    grad[t, c, strip(q)] += from_right[t, c, q]
                    left_copy(t, c, q).start()
        if t == 0:
            for d in range(1, n):
                peak_copy(d).wait_recv()
        else:
            for c in range(2):
                hand_over(t - 1, c)
        peak = peaks[0, t]
        for d in range(1, n):
            peak = peak + peaks[d, t]
        mean_peak = jnp.broadcast_to((peak / led_total)[:1, :1], (rows, length))
        for c in range(2):
            @pl.when(z > 0)
            def _():
                right_copy(t, c, z).wait_recv()
                grad[t, c, strip(z)] += from_left[t, c, z]

            @pl.when(z < n - 1)
            def _():
                left_copy(t, c, z).wait_recv()
                grad[t, c, strip(z)] += from_right[t, c, z]

            gathered[me, t, c] = pupils_ref[t, c, strip(z)] + grad[t, c, strip(z)] / mean_peak
            for j in (1, *range(2, m, 2)):
                tile_copy(t, c, j).start()
        if t == 0:
            mix = mixed_rows()
            for k in range(later, tl * per_tile):
                push(k)

    for t in range(tl - 1):
        for c in range(2):
            mix_in(t, c)
    for c in range(2):
        hand_over(tl - 1, c)
    for c in range(2):
        mix_in(tl - 1, c)

    for d in range(1, m):
        place_copy(d).wait_send()
    for d in range(1, n):
        peak_copy(d).wait_send()
    for t in range(tl):
        for c in range(2):
            for d in range(1, m):
                tile_copy(t, c, d).wait_send()
            for d in range(1, n):
                @pl.when(jnp.logical_and(z > 0, z + d < n))
                def _():
                    right_copy(t, c, z + d).wait_send()

                @pl.when(jnp.logical_and(z < n - 1, z - d >= 0))
                def _():
                    left_copy(t, c, z - d).wait_send()
    for k in range(max(tl * per_tile - FLIGHT, 0), tl * per_tile):
        for side, end in ((0, 0), (1, n - 1)):
            @pl.when(z == end)
            def _():
                end_copy(k, side).wait_send()


def per_device(n, m, spectra, pupils, amplitudes, offsets, positions):
    tl, leds = amplitudes.shape[:2]
    length = pupils.shape[2]
    rows = length // n
    vmem = pl.BlockSpec(memory_space=pltpu.VMEM)
    hbm = pl.BlockSpec(memory_space=pltpu.HBM)
    first, second = (jnp.asarray(table) for table in inverse_tables(length))
    operands = (spectra, pupils, amplitudes, offsets, positions, first, second)
    dma = pltpu.SemaphoreType.DMA
    strips = pltpu.VMEM((tl, 2, n, rows, length), jnp.float32)
    return pl.pallas_call(
        functools.partial(kernel, n, m, leds * n),
        out_shape=jax.ShapeDtypeStruct((tl, 2, rows, length), jnp.float32),
        in_specs=[hbm] * 7,
        out_specs=vmem,
        scratch_shapes=[
            *[
                (pltpu.SMEM if each.dtype == jnp.int32 else pltpu.VMEM)(each.shape, each.dtype)
                for each in operands
            ],
            dma((4 + 3 * tl,)),
            pltpu.VMEM((leds, 2 * length, length), jnp.bfloat16),
            pltpu.VMEM((leds, length, 2 * length), jnp.bfloat16),
            pltpu.VMEM((tl, 2, length, length), jnp.float32),
            strips,
            strips,
            pltpu.VMEM((n, tl, 8, 128), jnp.float32),
            pltpu.VMEM((m, 8, 128), jnp.float32),
            pltpu.VMEM((m, tl, 2, rows, length), jnp.float32),
            dma((n,)), dma((n,)), dma((m,)), dma((m,)),
            dma((tl, 2, n)), dma((tl, 2, n)), dma((tl, 2, n)), dma((tl, 2, n)),
            dma((tl, 2, m)), dma((tl, 2, m)),
        ],
        compiler_params=pltpu.CompilerParams(
            collective_id=0, has_side_effects=True, vmem_limit_bytes=60 << 20
        ),
    )(*operands)


def solution(mesh):
    placed = (
        P(("groups", "tile"), None, None, None),
        P(("groups", "tile"), None, None, None),
        P(("groups", "tile"), "led", None, None),
        P(("groups", "tile"), "led", None),
        P(("groups", "tile"), None),
    )
    return jax.shard_map(
        functools.partial(per_device, mesh.shape["led"], mesh.shape["tile"]),
        mesh=mesh,
        in_specs=placed,
        out_specs=P(("groups", "tile"), None, "led", None),
        check_vma=False,
    )
```
